512 devices in a mesh: blk: 32 (over z_hi, y, x), freq: 16 (over z_lo, core).
Axes of the slice: x: 4, y: 4, z: 16 (z_hi: 2, z_lo: 8; z = z_hi * 8 + z_lo), core: 2. Of those that a mesh axis runs over, the one named last changes fastest.
Arguments:
- traces: bfloat16 [1024, 1024, 1024], P('blk', 'freq'), as said below
- mute: int32 [1024, 1024], P('blk', 'freq'), may hold values from 0 to 127, as said below
- operator: bfloat16 [2, 32, 1024, 1024], P(None, 'freq', 'blk'), may hold values from -0.125 to 0.125
- wavelet: float32 [2, 32], replicated, may hold values from -40 to 40
Outputs:
- gradient: float32 [2, 32, 1024, 1024], P(None, 'freq', 'blk')
The draws below stay inside these ranges and needn't reach their ends.
Inputs may be any that keep to these rules, and one draw needn't show every extreme that they name: traces[s, r, t] == traces[r, s, t] for all shots s and receivers r (reciprocity). mute[s, r] == mute[r, s]; the largest value is reached in every draw.
All inputs are finite; a program needn't handle non-finite values.
Results may differ from the reference program's by a relative error of at most 0.0041.
Values may be sent and summed in bfloat16 or wider, within the bound.
A program may use at most 64 MiB of HBM per device.

```python
import math
import jax
import jax.numpy as jnp
from jax import lax

STATIONS = 1024
SAMPLES = 1024
LOW_FREQ = 8
MUTE_MAX = 128
NF = 32


def draw_traces(key, part):
    key = jax.random.fold_in(key, 11)
    columns = jnp.arange(STATIONS, dtype=jnp.int32)

    def pair_values(first, second):
        lower = jnp.minimum(first, second)
        upper = jnp.maximum(first, second)
        pair_key = jax.random.fold_in(jax.random.fold_in(key, lower), upper)
        return jnp.clip(jax.random.normal(pair_key, (SAMPLES,), jnp.float32), -6.0, 6.0)

    def shot_row(first):
        values = jax.vmap(lambda second: pair_values(first, second))(columns)
        return values.astype(jnp.bfloat16)
    return lax.map(shot_row, columns)


def draw_mute(key, part):
    key = jax.random.fold_in(key, 23)
    starts = jax.random.randint(key, (STATIONS, STATIONS), 0, MUTE_MAX, dtype=jnp.int32)
    starts = jnp.maximum(starts, starts.T)
    starts = starts.at[0, 1].set(MUTE_MAX - 1).at[1, 0].set(MUTE_MAX - 1)
    return starts.at[0, 0].set(0)


def level_of(rng, dims, cuts, least, largest):
    def one(axis_at, parts):
        heights = jax.random.uniform(jax.random.fold_in(jax.random.fold_in(rng, 6), axis_at), (parts,), jnp.float32, least / len(cuts), largest / len(cuts))
        return jnp.repeat(jnp.exp(heights), dims[axis_at] // parts).reshape((-1,) + (1,) * (len(dims) - axis_at - 1))

    level = one(*cuts[0])
    for cut in cuts[1:]:
        level = level * one(*cut)
    return level


def noise(rng, shape, scale, reach, pieces=(), kind=jnp.bfloat16):
    drawn = jax.random.normal(rng, shape, jnp.float32) * scale
    if len(pieces) > 0:
        drawn = level_of(rng, shape, pieces, -0.22, 0.18) * drawn
    return jnp.clip(drawn, min=-reach, max=reach).astype(kind)


def setup_inputs(seed: int = 0) -> dict:
    keys = jax.random.split(jax.random.key(seed), 5)
    return {
        "traces": draw_traces(jax.random.fold_in(keys[4], 71), 0),
        "mute": draw_mute(jax.random.fold_in(keys[4], 71), 0),
        "operator": noise(keys[2], (2, NF, STATIONS, STATIONS), (2 * STATIONS) ** -0.5, 0.125, ((1, 16), (2, 32))),
        "wavelet": noise(keys[3], (2, NF), 8.0, 40.0, (), jnp.float32),
    }


def band_table():
    times = jnp.arange(SAMPLES, dtype=jnp.int32)
    freqs = LOW_FREQ + jnp.arange(NF, dtype=jnp.int32)
    phase = times[:, None] * freqs[None, :] % SAMPLES
    angle = phase.astype(jnp.float32) * (2.0 * math.pi / SAMPLES)
    factor = 1.0 / math.sqrt(SAMPLES)
    return jnp.concatenate([jnp.cos(angle) * factor, -jnp.sin(angle) * factor], axis=1).astype(jnp.bfloat16)

def product(left, right):
    return jnp.dot(left, right, preferred_element_type=jnp.float32)

def reference(traces, mute, operator, wavelet):
    table = band_table()
    times = jnp.arange(SAMPLES, dtype=jnp.int32)

    def shot_spectrum(inputs):
        row, starts = inputs
        muted = jnp.where(times[None, :] >= starts[:, None], row, jnp.zeros_like(row))
        return product(muted, table).astype(jnp.bfloat16)
    spectra = lax.map(shot_spectrum, (traces, mute))
    spectra = spectra.reshape(STATIONS, STATIONS, 2, NF).transpose(2, 3, 0, 1)
    factor = 1.0 / math.sqrt(STATIONS)

    def one_frequency(inputs):
        pmat, xmat, wave = inputs
        conv_re = product(pmat[0], xmat[0]) - product(pmat[1], xmat[1])
        conv_im = product(pmat[0], xmat[1]) + product(pmat[1], xmat[0])
        xre = xmat[0].astype(jnp.float32)
        xim = xmat[1].astype(jnp.float32)
        res_re = pmat[0].astype(jnp.float32) - (wave[0] * xre - wave[1] * xim) + conv_re
        res_im = pmat[1].astype(jnp.float32) - (wave[0] * xim + wave[1] * xre) + conv_im
        resid = jnp.stack([res_re, res_im]).astype(jnp.bfloat16)
        corr_re = product(pmat[0], resid[0]) + product(pmat[1], resid[1])
        corr_im = product(pmat[0], resid[1]) - product(pmat[1], resid[0])
        rre = resid[0].astype(jnp.float32)
        rim = resid[1].astype(jnp.float32)
        grad_re = (corr_re - (wave[0] * rre + wave[1] * rim)) * factor
        grad_im = (corr_im - (wave[0] * rim - wave[1] * rre)) * factor
        return jnp.stack([grad_re, grad_im])
    result = lax.map(one_frequency, (spectra.transpose(1, 0, 2, 3), operator.transpose(1, 0, 2, 3), wavelet.T))
    return result.transpose(1, 0, 2, 3)
```

```python
import functools
import math

import jax
import jax.numpy as jnp
import numpy as np
from jax import lax
from jax.experimental import pallas as pl
from jax.experimental.pallas import tpu as pltpu
from jax.sharding import PartitionSpec as P

LOW_FREQ = 8
MESH = pl.DeviceIdType.MESH
BF16 = jnp.bfloat16
F32 = jnp.float32

OFFSETS = (0, 1, 3, 6, 4)


def div(a, b):
    return lax.div(a, jnp.int32(b))


def rem(a, b):
    return lax.rem(a, jnp.int32(b))


def band_table(samples, count):
    times = np.arange(samples, dtype=np.int64)
    freqs = LOW_FREQ + np.arange(count, dtype=np.int64)
    phase = times[:, None] * freqs[None, :] % samples
    angle = phase.astype(np.float32) * np.float32(2.0 * math.pi / samples)
    factor = np.float32(1.0 / math.sqrt(samples))
    table = np.concatenate([np.cos(angle) * factor, -np.sin(angle) * factor], axis=1)
    return np.ascontiguousarray(table.T).astype(jnp.bfloat16)


def swap(x):
    return pltpu.roll(x, 64, 1)


def low_half(rows):
    return lax.broadcasted_iota(jnp.int32, (rows, 128), 1) < 64


def kernel(
    table, traces, mute, oper, wave, got,
    tr, zs, zb, pin, pk, xs, xp, w, y, res, gs,
    tr_sem, zsend, zrecv, xsend, xrecv, gsend, grecv, psend, precv,
):
    b = lax.axis_index("blk").astype(jnp.int32)
    f = lax.axis_index("freq").astype(jnp.int32)
    h, xy = div(b, 16), rem(b, 16)
    yy, xx = div(xy, 4), rem(xy, 4)
    l, core = div(f, 2), rem(f, 2)
    z = h * 8 + l
    u = h * 4 + yy
    d = rem(l - u + 8, 8)
    kept = (d == 0) | (d == 1) | (d == 3) | (d == 6) | ((d == 4) & (h == 0))
    slot = jnp.where(d == 1, 1, 0) + jnp.where(d == 3, 2, 0) + jnp.where(d == 6, 3, 0) + jnp.where(d == 4, 4, 0) + 5 * h
    far = rem(l + 4, 8)
    far_f = far * 2 + core
    part = rem(1 + h + div(l, 4), 2)
    mine = far * 4 + core * 2 + part

    def load(ch):
        return pltpu.make_async_copy(traces.at[pl.ds(8 * ch, 8)], tr.at[pl.ds(8 * ch, 8)], tr_sem.at[ch])

    @pl.when(kept)
    def _():
        for ch in range(4):
            load(ch).start()

    barrier = pltpu.get_barrier_semaphore()
    me = z * 2 + core

    def ring_of(i):
        t = rem(me + i, 32)
        to_z, to_core = div(t, 2), rem(t, 2)
        to_h, to_l = div(to_z, 8), rem(to_z, 8)
        return to_h, to_l, to_core

    def greet_ring(i, carry):
        to_h, to_l, to_core = ring_of(i)
        pl.semaphore_signal(barrier, inc=1, device_id=(to_h * 16 + xy, to_l * 2 + to_core), device_id_type=MESH)
        return carry

    def greet_far(i, carry):
        pl.semaphore_signal(barrier, inc=1, device_id=(i, far_f), device_id_type=MESH)
        return carry

    lax.fori_loop(1, 32, greet_ring, 0)
    lax.fori_loop(0, 32, greet_far, 0)

    def near(dy, dx):
        return h * 16 + rem(yy + dy + 4, 4) * 4 + rem(xx + dx + 4, 4)

    for dy, dx in ((0, 1), (0, -1), (1, 0), (-1, 0)):
        pl.semaphore_signal(barrier, inc=1, device_id=(near(dy, dx), f), device_id_type=MESH)

    lo32 = low_half(32)
    for a in range(2):
        for m in range(8):
            re = oper[0, a, :, 128 * m : 128 * m + 128].astype(F32)
            im = oper[1, a, :, 128 * m : 128 * m + 128].astype(F32)
            xs[a, 2 * m] = jnp.where(lo32, re, swap(im)).astype(BF16)
            xs[a, 2 * m + 1] = jnp.where(lo32, swap(re), im).astype(BF16)

    @pl.when(kept)
    def _():
        eye = (lax.broadcasted_iota(jnp.int32, (64, 64), 0) == lax.broadcasted_iota(jnp.int32, (64, 64), 1)).astype(F32)
        ones = jnp.ones((64, 128), BF16)
        lane = lax.broadcasted_iota(jnp.int32, (512, 128), 1).astype(F32)
        for ch in range(4):
            starts = [
                (eye * mute[8 * ch + s : 8 * ch + s + 1, :].astype(F32)).astype(BF16) for s in range(8)
            ]
            first = jnp.dot(jnp.concatenate(starts, axis=0), ones, preferred_element_type=F32)
            load(ch).wait()
            head = tr[8 * ch : 8 * ch + 8, :, 0:128].astype(F32).reshape(512, 128)
            head = jnp.where(lane >= first, head, 0.0).astype(BF16)
            tr[8 * ch : 8 * ch + 8, :, 0:128] = head.reshape(8, 64, 128)
            spec = lax.dot_general(
                table[...], tr[8 * ch : 8 * ch + 8].reshape(512, 1024), (((1,), (1,)), ((), ())),
                preferred_element_type=F32,
            )
            for p in range(4):
                re = spec[0:32, 128 * p : 128 * p + 128]
                im = spec[32:64, 128 * p : 128 * p + 128]
                even = jnp.where(lo32, re, swap(im))
                odd = jnp.where(lo32, swap(re), im)
                s = 8 * ch + 2 * p
                for jt in range(4):
                    zs[pl.ds(jt * 256 + s, 8, stride=32), :] = even[8 * jt : 8 * jt + 8]
                    zs[pl.ds(jt * 256 + s + 1, 8, stride=32), :] = odd[8 * jt : 8 * jt + 8]
        zb[...] = zs[...].astype(BF16)

    pl.semaphore_wait(barrier, 67)

    def freq_of(to_h, to_l, to_core):
        return rem(to_l + 4, 8) * 4 + to_core * 2 + rem(1 + to_h + div(to_l, 4), 2)

    @pl.when(kept)
    def _():
        own = pltpu.make_async_copy(
            zb.at[pl.ds(pl.multiple_of(mine * 32, 32), 32)], pin.at[slot * 2 + core], zrecv
        )
        own.start()

        def send(i, carry):
            to_h, to_l, to_core = ring_of(i)
            j = freq_of(to_h, to_l, to_core)
            pltpu.make_async_remote_copy(
                src_ref=zb.at[pl.ds(pl.multiple_of(j * 32, 32), 32)],
                dst_ref=pin.at[slot * 2 + core],
                send_sem=zsend,
                recv_sem=zrecv,
                device_id=(to_h * 16 + xy, to_l * 2 + to_core),
                device_id_type=MESH,
            ).start()
            return carry

        lax.fori_loop(1, 32, send, 0)

    def send_oper(i, carry):
        a, to_xy = rem(i, 2), rem(xy + div(i, 2), 16)
        to_h = rem(a + 1 + div(far, 4), 2)
        pltpu.make_async_remote_copy(
            src_ref=xs.at[a, to_xy],
            dst_ref=xp.at[pl.ds(pl.multiple_of(b * 32, 32), 32)],
            send_sem=xsend,
            recv_sem=xrecv,
            device_id=(to_h * 16 + to_xy, far_f),
            device_id_type=MESH,
        ).start()
        return carry

    lax.fori_loop(0, 32, send_oper, 0)

    pltpu.make_async_copy(pin, pin, zrecv).wait()
    for k in range(9):
        left, right = pin[2 * k].astype(F32), pin[2 * k + 1].astype(F32)
        pk[xy, 2 * k] = jnp.where(lo32, left, swap(right)).astype(BF16)
        pk[xy, 2 * k + 1] = jnp.where(lo32, swap(left), right).astype(BF16)

    def place(axis, first, second):
        return (second, first) if axis == 0 else (first, second)

    def owner(axis, first, second):
        dy, dx = place(axis, first, second)
        return rem(yy + dy + 4, 4) * 4 + rem(xx + dx + 4, 4)

    def copy(axis, ring, step, panel, start, size, sem):
        dy, dx = place(axis, *((step, 0) if ring == 0 else (0, step)))
        rows = pk.at[owner(axis, *panel), pl.ds(start, size)]
        return pltpu.make_async_remote_copy(
            src_ref=rows, dst_ref=rows, send_sem=psend, recv_sem=precv.at[axis * 20 + sem],
            device_id=(near(dy, dx), f), device_id_type=MESH,
        )

    def arrived(axis, panel, start, size, sem):
        rows = pk.at[owner(axis, *panel), pl.ds(start, size)]
        pltpu.make_async_copy(rows, rows, precv.at[axis * 20 + sem]).wait()

    spans = ((0, 10, 5), (10, 8, 4))

    def out_second(axis, q, at):
        start, size, _ = spans[axis]
        copy(axis, 1, 1, (q, 0), start, size, 4 + 4 * at).start()
        copy(axis, 1, -1, (q, 0), start, size, 5 + 4 * at).start()

    for axis in range(2):
        start, size, half = spans[axis]
        copy(axis, 0, 1, (0, 0), start, size, 0).start()
        copy(axis, 0, -1, (0, 0), start, size, 1).start()
    for axis in range(2):
        out_second(axis, 0, 0)
    for axis in range(2):
        start, size, half = spans[axis]
        arrived(axis, (-1, 0), start, size, 0)
        copy(axis, 0, 1, (-1, 0), start, half, 2).start()
        arrived(axis, (1, 0), start, size, 1)
        copy(axis, 0, -1, (1, 0), start + half, half, 3).start()
    for axis in range(2):
        out_second(axis, -1, 1)
        out_second(axis, 1, 2)
    for axis in range(2):
        start, size, half = spans[axis]
        arrived(axis, (2, 0), start, half, 2)
        arrived(axis, (2, 0), start + half, half, 3)
        out_second(axis, 2, 3)
    for at, q in enumerate((0, -1, 1, 2)):
        for axis in range(2):
            start, size, half = spans[axis]
            arrived(axis, (q, -1), start, size, 4 + 4 * at)
            copy(axis, 1, 1, (q, -1), start, half, 6 + 4 * at).start()
            arrived(axis, (q, 1), start, size, 5 + 4 * at)
            copy(axis, 1, -1, (q, 1), start + half, half, 7 + 4 * at).start()
    for at, q in enumerate((0, -1, 1, 2)):
        for axis in range(2):
            start, size, half = spans[axis]
            arrived(axis, (q, 2), start, half, 6 + 4 * at)
            arrived(axis, (q, 2), start + half, half, 7 + 4 * at)

    for row in range(8):
        for k in range(5 if row < 4 else 4):
            col = (row + OFFSETS[k]) % 8
            for c in range(2):
                tile = jnp.concatenate(
                    [pk[4 * (row % 4) + x, 2 * (k + 5 * (row // 4)) + c] for x in range(4)], axis=0
                )
                w[128 * row : 128 * row + 128, 256 * col + 128 * c : 256 * col + 128 * c + 128] = tile
                if col != row:
                    w[128 * col : 128 * col + 128, 256 * row + 128 * c : 256 * row + 128 * c + 128] = tile.T

    pltpu.make_async_copy(xp, xp, xrecv).wait()
    lo = low_half(128)
    lane = lax.broadcasted_iota(jnp.int32, (128, 128), 1)
    row_at = lax.broadcasted_iota(jnp.int32, (128, 128), 0)
    for v in range(8):
        x = xp[128 * v : 128 * v + 128].astype(F32)
        sx = swap(x)
        y[256 * v : 256 * v + 128, 0:128] = x.astype(BF16)
        y[256 * v + 128 : 256 * v + 256, 0:128] = jnp.where(lo, -sx, sx).astype(BF16)
        here = row_at + (128 * v - 64 * xy)
        y[256 * v : 256 * v + 128, 128:256] = jnp.where(lo & (lane == here), 1.0, 0.0).astype(BF16)
        y[256 * v + 128 : 256 * v + 256, 128:256] = jnp.where(
            (lane >= 64) & (lane - 64 == here), 1.0, 0.0
        ).astype(BF16)
    qr, qi = wave[0, mine], wave[1, mine]
    lo256 = low_half(256)
    for m in range(4):
        rows = slice(256 * m, 256 * m + 256)
        conv = jnp.dot(w[rows], y[...], preferred_element_type=F32)
        x = xp[rows].astype(F32)
        sx = swap(x)
        r = conv[:, 128:256] - (qr * x + qi * jnp.where(lo256, -sx, sx)) + conv[:, 0:128]
        res[rows] = r.astype(BF16)

    for v in range(8):
        r = res[128 * v : 128 * v + 128].astype(F32)
        sr = swap(r)
        y[256 * v : 256 * v + 128, 0:128] = r.astype(BF16)
        y[256 * v + 128 : 256 * v + 256, 0:128] = jnp.where(lo, sr, -sr).astype(BF16)
    for m in range(4):
        rows = slice(256 * m, 256 * m + 256)
        corr = jnp.dot(w[rows], y[:, 0:128], preferred_element_type=F32)
        r = res[rows].astype(F32)
        sr = swap(r)
        g = (corr - (qr * r + qi * jnp.where(lo256, sr, -sr))) * (1.0 / 32.0)
        gs[rows] = g.astype(BF16)

        def send_back(i, carry):
            to = 8 * m + i
            pltpu.make_async_remote_copy(
                src_ref=gs.at[pl.ds(pl.multiple_of(to * 32, 32), 32)],
                dst_ref=got.at[part, xy],
                send_sem=gsend,
                recv_sem=grecv,
                device_id=(to, far_f),
                device_id_type=MESH,
            ).start()
            return carry

        lax.fori_loop(0, 8, send_back, 0)

    @pl.when(kept)
    def _():
        sent = zb.at[pl.ds(0, 992)]
        pltpu.make_async_copy(sent, sent, zsend).wait()

    pltpu.make_async_copy(xs, xs, xsend).wait()
    for axis in range(2):
        _, size, half = spans[axis]
        for count, part_size in ((10, size), (10, half)):
            for i in range(count):
                rows = pk.at[0, pl.ds(0, part_size)]
                pltpu.make_async_copy(rows, rows, psend).wait()
    pltpu.make_async_copy(gs, gs, gsend).wait()
    pltpu.make_async_copy(got, got, grecv).wait()


def unpack(got, out):
    lo = low_half(32)
    for a in range(2):
        for m in range(8):
            left, right = got[a, 2 * m].astype(F32), got[a, 2 * m + 1].astype(F32)
            out[0, a, :, 128 * m : 128 * m + 128] = jnp.where(lo, left, swap(right))
            out[1, a, :, 128 * m : 128 * m + 128] = jnp.where(lo, swap(left), right)


def body(traces, mute, operator, wavelet):
    table = jnp.asarray(band_table(1024, 32))
    vmem = pl.BlockSpec(memory_space=pltpu.VMEM)
    dma = pltpu.SemaphoreType.DMA
    got = pl.pallas_call(
        kernel,
        out_shape=jax.ShapeDtypeStruct((2, 16, 32, 128), BF16),
        in_specs=[vmem, pl.BlockSpec(memory_space=pl.ANY), vmem, vmem, pl.BlockSpec(memory_space=pltpu.SMEM)],
        out_specs=vmem,
        scratch_shapes=[
            pltpu.VMEM((32, 64, 1024), BF16),
            pltpu.VMEM((1024, 128), F32),
            pltpu.VMEM((1024, 128), BF16),
            pltpu.VMEM((18, 32, 128), BF16),
            pltpu.VMEM((16, 18, 32, 128), BF16),
            pltpu.VMEM((2, 16, 32, 128), BF16),
            pltpu.VMEM((1024, 128), BF16),
            pltpu.VMEM((1024, 2048), BF16),
            pltpu.VMEM((2048, 256), BF16),
            pltpu.VMEM((1024, 128), BF16),
            pltpu.VMEM((1024, 128), BF16),
            dma((4,)), dma, dma, dma, dma, dma, dma, dma, dma((40,)),
        ],
        compiler_params=pltpu.CompilerParams(
            collective_id=0, has_side_effects=True, vmem_limit_bytes=40 * 1024 * 1024
        ),
        cost_estimate=pl.CostEstimate(flops=1 << 30, bytes_accessed=5 << 20, transcendentals=0),
        name="evaluate",
    )(table, traces, mute, operator, wavelet)
    return pl.pallas_call(
        unpack,
        out_shape=jax.ShapeDtypeStruct((2, 2, 32, 1024), F32),
        in_specs=[vmem],
        out_specs=vmem,
        name="unpack",
    )(got)


def solution(mesh):
    in_specs = (P("blk", "freq", None), P("blk", "freq"), P(None, "freq", "blk", None), P())
    out_specs = P(None, "freq", "blk", None)
    return jax.shard_map(body, mesh=mesh, in_specs=in_specs, out_specs=out_specs, check_vma=False)
```

```python
import functools
import math

import jax
import jax.numpy as jnp
import numpy as np
from jax import lax
from jax.experimental import pallas as pl
from jax.experimental.pallas import tpu as pltpu
from jax.sharding import PartitionSpec as P

LOW_FREQ = 8
MESH = pl.DeviceIdType.MESH
BF16 = jnp.bfloat16
F32 = jnp.float32

OFFSETS = (0, 1, 3, 6, 4)


def div(a, b):
    return lax.div(a, jnp.int32(b))


def rem(a, b):
    return lax.rem(a, jnp.int32(b))


def wrap(a, n):
    return jnp.where(a >= n, a - n, a)


def frequency_at(device):
    z, core = device // 2, device % 2
    return (z % 8 + 4) % 8 * 4 + core * 2 + (1 + z // 8 + z % 8 // 4) % 2


def band_table(samples, count):
    times = np.arange(samples, dtype=np.int64)
    freqs = LOW_FREQ + np.array([frequency_at(t) for t in range(count)], dtype=np.int64)
    phase = times[:, None] * freqs[None, :] % samples
    angle = phase.astype(np.float32) * np.float32(2.0 * math.pi / samples)
    factor = np.float32(1.0 / math.sqrt(samples))
    table = np.concatenate([np.cos(angle) * factor, -np.sin(angle) * factor], axis=1)
    return np.ascontiguousarray(table.T).astype(jnp.bfloat16)


def swap(x):
    return pltpu.roll(x, 64, 1)


def low_half(rows):
    return lax.broadcasted_iota(jnp.int32, (rows, 128), 1) < 64


def kernel(
    table_in, traces, mute_in, oper_in, wave_in, got,
    table, mute, oper, wave, tr, zs, zb, pin, mid, pk, xs, xp, w, y, res, gs,
    in_sem, tr_sem, zsend, zrecv, xsend, xrecv, gsend, grecv, asend, arecv, bsend, brecv, csend, crecv,
):
    b = lax.axis_index("blk").astype(jnp.int32)
    f = lax.axis_index("freq").astype(jnp.int32)
    h, xy = div(b, 16), rem(b, 16)
    yy, xx = div(xy, 4), rem(xy, 4)
    l, core = div(f, 2), rem(f, 2)
    z = h * 8 + l
    u = h * 4 + yy
    d = rem(l - u + 8, 8)
    kept = (d == 0) | (d == 1) | (d == 3) | (d == 6) | ((d == 4) & (h == 0))
    slot = jnp.where(d == 1, 1, 0) + jnp.where(d == 3, 2, 0) + jnp.where(d == 6, 3, 0) + jnp.where(d == 4, 4, 0) + 5 * h
    far = rem(l + 4, 8)
    part = rem(1 + h + div(l, 4), 2)
    group = div(xx, 2)
    mine = far * 4 + group * 2 + part
    block = (yy * 2 + rem(xx, 2)) * 2 + core
    far_group = far * 2 + group

    def load(ch):
        return pltpu.make_async_copy(traces.at[pl.ds(8 * ch, 8)], tr.at[pl.ds(8 * ch, 8)], tr_sem.at[ch])

    @pl.when(kept)
    def _():
        load(0).start()

    inputs = [
        pltpu.make_async_copy(src, dst, in_sem.at[i])
        for i, (src, dst) in enumerate(((mute_in, mute), (table_in, table), (oper_in, oper), (wave_in, wave)))
    ]
    for c in inputs:
        c.start()

    @pl.when(kept)
    def _():
        for ch in range(1, 4):
            load(ch).start()

    barrier = pltpu.get_barrier_semaphore()

    def ring_device(to):
        return xy + jnp.where(to >= 8, 16, 0), wrap(to, 8) * 2 + core

    for half in range(2):
        for off in OFFSETS[: 5 - half]:
            to = 8 * half + wrap(yy + (4 * half + off) % 8, 8)

            @pl.when(to != z)
            def _():
                pl.semaphore_signal(barrier, inc=1, device_id=ring_device(to), device_id_type=MESH)

    at_y = [wrap(yy + i, 4) * 4 for i in range(4)]
    at_x = [wrap(xx + i, 4) for i in range(4)]

    def greet(device):
        pl.semaphore_signal(barrier, inc=1, device_id=device, device_id_type=MESH)

    def greet_far(i, carry):
        for half in range(2):
            for xl in range(2):
                to = 16 * half + 4 * i + xl
                greet((to + 2 * core, far * 2))
                greet((to + 2 * core, far * 2 + 1))
                greet((to + 2 - 2 * core, far_group))
        return carry

    lax.fori_loop(0, 4, greet_far, 0)

    def near(dy, dx, to_core):
        return h * 16 + at_y[dy] + at_x[dx], l * 2 + to_core

    greet(near(0, 0, 1 - core))
    for i in range(1, 4):
        greet(near(0, i, core))
        greet(near(i, 0, core))

    lo32 = low_half(32)
    for c in inputs:
        c.wait()
    for a in range(2):
        for m in range(8):
            re = oper[0, a, :, 128 * m : 128 * m + 128].astype(F32)
            im = oper[1, a, :, 128 * m : 128 * m + 128].astype(F32)
            xs[a, 2 * m] = jnp.where(lo32, re, swap(im)).astype(BF16)
            xs[a, 2 * m + 1] = jnp.where(lo32, swap(re), im).astype(BF16)

    @pl.when(kept)
    def _():
        eye = (lax.broadcasted_iota(jnp.int32, (64, 64), 0) == lax.broadcasted_iota(jnp.int32, (64, 64), 1)).astype(F32)
        ones = jnp.ones((64, 128), BF16)
        lane = lax.broadcasted_iota(jnp.int32, (512, 128), 1).astype(F32)
        for ch in range(4):
            starts = [
                (eye * mute[8 * ch + s : 8 * ch + s + 1, :].astype(F32)).astype(BF16) for s in range(8)
            ]
            first = jnp.dot(jnp.concatenate(starts, axis=0), ones, preferred_element_type=F32)
            load(ch).wait()
            head = tr[8 * ch : 8 * ch + 8, :, 0:128].astype(F32).reshape(512, 128)
            head = jnp.where(lane >= first, head, 0.0).astype(BF16)
            tr[8 * ch : 8 * ch + 8, :, 0:128] = head.reshape(8, 64, 128)
            spec = lax.dot_general(
                table[...], tr[8 * ch : 8 * ch + 8].reshape(512, 1024), (((1,), (1,)), ((), ())),
                preferred_element_type=F32,
            )
            for p in range(4):
                re = spec[0:32, 128 * p : 128 * p + 128]
                im = spec[32:64, 128 * p : 128 * p + 128]
                even = jnp.where(lo32, re, swap(im))
                odd = jnp.where(lo32, swap(re), im)
                s = 8 * ch + 2 * p
                for jt in range(4):
                    zs[pl.ds(jt * 256 + s, 8, stride=32), :] = even[8 * jt : 8 * jt + 8]
                    zs[pl.ds(jt * 256 + s + 1, 8, stride=32), :] = odd[8 * jt : 8 * jt + 8]
        zb[...] = zs[...].astype(BF16).reshape(32, 32, 128)

    @pl.when(kept)
    def _():
        pl.semaphore_wait(barrier, 70)

    @pl.when(jnp.logical_not(kept))
    def _():
        pl.semaphore_wait(barrier, 55)


    @pl.when(kept)
    def _():
        def send(to):
            pltpu.make_async_remote_copy(
                src_ref=zb.at[pl.ds(2 * to, 2)], dst_ref=pin.at[:, slot], send_sem=zsend, recv_sem=zrecv,
                device_id=ring_device(to), device_id_type=MESH,
            ).start()

        def send_two(i, carry):
            send(wrap(z + 7 - i, 16))
            send(wrap(z + 9 + i, 16))
            return carry

        send(wrap(z + 8, 16))
        lax.fori_loop(0, 7, send_two, 0)
        pltpu.make_async_copy(zb.at[pl.ds(2 * z, 2)], pin.at[:, slot], zrecv).start()

    to_half = [16 * rem(a + 1 + div(far, 4), 2) for a in range(2)]

    def send_oper():
        for i in range(4):
            for xl in range(2):
                for k in range(2):
                    for a in range(2):
                        pltpu.make_async_remote_copy(
                            src_ref=xs.at[a, at_y[i] + 2 * xl + k],
                            dst_ref=xp.at[pl.ds(pl.multiple_of(b * 32, 32), 32)],
                            send_sem=xsend,
                            recv_sem=xrecv,
                            device_id=(to_half[a] + at_y[i] + 2 * core + xl, far * 2 + k),
                            device_id_type=MESH,
                        ).start()

    def move(src, dst, send_sem, recv_sem, device):
        pltpu.make_async_remote_copy(
            src_ref=src, dst_ref=dst, send_sem=send_sem, recv_sem=recv_sem, device_id=device, device_id_type=MESH
        ).start()

    def arrived(ref, sem):
        pltpu.make_async_copy(ref, ref, sem).wait()

    def to_group(src, dst, send_sem, recv_sem):
        for which in range(2):
            for xl in range(2):
                to_x = 2 * which + xl

                @pl.when(xx != to_x)
                def _():
                    move(src.at[which], dst, send_sem, recv_sem, (h * 16 + at_y[0] + to_x, f))

                @pl.when(xx == to_x)
                def _():
                    pltpu.make_async_copy(src.at[which], dst, recv_sem).start()

    def fill(k):
        for row in range(8):
            for n in range(5 - row // 4):
                col = (row + OFFSETS[n]) % 8
                tile = jnp.concatenate([pk[row % 4, k, x, n + 5 * (row // 4)] for x in range(4)], axis=0)
                for c in range(2):
                    at = 256 * col + 128 * c + 64 * k
                    w[128 * row : 128 * row + 128, at : at + 64] = tile[:, 64 * c : 64 * c + 64]
                if col != row:
                    turned = tile.T
                    for c in range(2):
                        w[128 * col + 64 * k : 128 * col + 64 * k + 64, 256 * row + 128 * c : 256 * row + 128 * c + 128] = (
                            turned[64 * c : 64 * c + 64]
                        )

    arrived(pin, zrecv)

    @pl.when(core == 0)
    def _():
        to_group(pin, pk.at[yy, 0, xx], asend, arecv.at[yy, xx])
        for i in (2, 1, 3):
            move(pin.at[group], pk.at[yy, 0, xx], asend, arecv.at[yy, xx], near(i, 0, 0))

    @pl.when(core == 1)
    def _():
        for i in (2, 1, 3):
            move(pin, mid.at[yy], bsend, brecv.at[yy], near(i, 0, 1))
        to_group(pin, pk.at[yy, 1, xx], asend, arecv.at[yy, xx])

    send_oper()
    def pass_on(row, k):
        for x in range(4):
            arrived(pk.at[row, k, x], arecv.at[row, x])
        rows = pk.at[row, k]
        move(rows, rows, csend, crecv.at[row], near(0, 0, 1 - k))

    others = [div(at_y[i], 4) for i in (1, 3, 2)]

    @pl.when(core == 0)
    def _():
        for n in (1, 3, 2):
            x = at_x[n]
            panel = pk.at[yy, 0, x]
            arrived(panel, arecv.at[yy, x])
            for i in (2, 1, 3):
                move(panel, panel, asend, arecv.at[yy, x], near(i, 0, 0))
        arrived(pk.at[yy, 0, xx], arecv.at[yy, xx])
        move(pk.at[yy, 0], pk.at[yy, 0], csend, crecv.at[yy], near(0, 0, 1))
        for row in others:
            pass_on(row, 0)
        fill(0)
        for row in range(4):
            arrived(pk.at[row, 1], crecv.at[row])
        fill(1)

    @pl.when(core == 1)
    def _():
        for row in others:
            arrived(mid.at[row], brecv.at[row])
            to_group(mid.at[row], pk.at[row, 1, xx], asend, arecv.at[row, xx])
        for row in [yy, *others]:
            pass_on(row, 1)
        fill(1)
        for row in range(4):
            arrived(pk.at[row, 0], crecv.at[row])
        fill(0)

    pltpu.make_async_copy(xp, xp, xrecv).wait()
    lo = low_half(128)
    lane = lax.broadcasted_iota(jnp.int32, (128, 128), 1)
    row_at = lax.broadcasted_iota(jnp.int32, (128, 128), 0)
    for v in range(8):
        x = xp[128 * v : 128 * v + 128].astype(F32)
        sx = swap(x)
        y[256 * v : 256 * v + 128, 0:128] = x.astype(BF16)
        y[256 * v + 128 : 256 * v + 256, 0:128] = jnp.where(lo, -sx, sx).astype(BF16)
        here = row_at + (128 * v - 64 * block)
        y[256 * v : 256 * v + 128, 128:256] = jnp.where(lo & (lane == here), 1.0, 0.0).astype(BF16)
        y[256 * v + 128 : 256 * v + 256, 128:256] = jnp.where(
            (lane >= 64) & (lane - 64 == here), 1.0, 0.0
        ).astype(BF16)
    qr, qi = wave[0, mine], wave[1, mine]
    lo256 = low_half(256)
    for m in range(4):
        rows = slice(256 * m, 256 * m + 256)
        conv = jnp.dot(w[rows], y[...], preferred_element_type=F32)
        x = xp[rows].astype(F32)
        sx = swap(x)
        r = conv[:, 128:256] - (qr * x + qi * jnp.where(lo256, -sx, sx)) + conv[:, 0:128]
        res[rows] = r.astype(BF16)

    for v in range(8):
        r = res[128 * v : 128 * v + 128].astype(F32)
        sr = swap(r)
        y[256 * v : 256 * v + 128, 0:128] = r.astype(BF16)
        y[256 * v + 128 : 256 * v + 256, 0:128] = jnp.where(lo, sr, -sr).astype(BF16)
    for half in range(2):
        for at in (512 * half, 512 * half + 256):
            rows = slice(at, at + 256)
            corr = jnp.dot(w[rows], y[:, 0:128], preferred_element_type=F32)
            r = res[rows].astype(F32)
            sr = swap(r)
            g = (corr - (qr * r + qi * jnp.where(lo256, sr, -sr))) * (1.0 / 32.0)
            gs[rows] = g.astype(BF16)

        def send_back(i, carry):
            to = 16 * half + wrap(xy + i, 16)
            pltpu.make_async_remote_copy(
                src_ref=gs.at[pl.ds(pl.multiple_of(to * 32, 32), 32)],
                dst_ref=got.at[part, block],
                send_sem=gsend,
                recv_sem=grecv,
                device_id=(to, far_group),
                device_id_type=MESH,
            ).start()
            return carry

        lax.fori_loop(0, 16, send_back, 0)

    @pl.when(kept)
    def _():
        sent = zb.at[pl.ds(0, 30)]
        pltpu.make_async_copy(sent, sent, zsend).wait()

    pltpu.make_async_copy(xs, xs, xsend).wait()
    def left(ref, sem, times):
        for _ in range(times):
            pltpu.make_async_copy(ref, ref, sem).wait()

    left(pin.at[0], asend, 12)
    left(pk.at[0, 0], csend, 4)

    @pl.when(core == 0)
    def _():
        left(pin.at[0], asend, 3)

    @pl.when(core == 1)
    def _():
        left(pin, bsend, 3)

    pltpu.make_async_copy(gs, gs, gsend).wait()
    pltpu.make_async_copy(got, got, grecv).wait()


def unpack(got, out):
    lo = low_half(32)
    for a in range(2):
        for m in range(8):
            left, right = got[a, 2 * m].astype(F32), got[a, 2 * m + 1].astype(F32)
            out[0, a, :, 128 * m : 128 * m + 128] = jnp.where(lo, left, swap(right))
            out[1, a, :, 128 * m : 128 * m + 128] = jnp.where(lo, swap(left), right)


def body(traces, mute, operator, wavelet):
    table = jnp.asarray(band_table(1024, 32))
    vmem = pl.BlockSpec(memory_space=pltpu.VMEM)
    dma = pltpu.SemaphoreType.DMA
    got = pl.pallas_call(
        kernel,
        out_shape=jax.ShapeDtypeStruct((2, 16, 32, 128), BF16),
        in_specs=[pl.BlockSpec(memory_space=pltpu.HBM)] * 5,
        out_specs=vmem,
        scratch_shapes=[
            pltpu.VMEM((64, 1024), BF16),
            pltpu.VMEM((32, 64), jnp.int32),
            pltpu.VMEM((2, 2, 32, 1024), BF16),
            pltpu.SMEM((2, 32), F32),
            pltpu.VMEM((32, 64, 1024), BF16),
            pltpu.VMEM((1024, 128), F32),
            pltpu.VMEM((32, 32, 128), BF16),
            pltpu.VMEM((2, 9, 32, 128), BF16),
            pltpu.VMEM((4, 2, 9, 32, 128), BF16),
            pltpu.VMEM((4, 2, 4, 9, 32, 128), BF16),
            pltpu.VMEM((2, 16, 32, 128), BF16),
            pltpu.VMEM((1024, 128), BF16),
            pltpu.VMEM((1024, 2048), BF16),
            pltpu.VMEM((2048, 256), BF16),
            pltpu.VMEM((1024, 128), BF16),
            pltpu.VMEM((1024, 128), BF16),
            dma((4,)), dma((4,)), dma, dma, dma, dma, dma, dma,
            dma, dma((4, 4)), dma, dma((4,)), dma, dma((4,)),
        ],
        compiler_params=pltpu.CompilerParams(
            collective_id=0, has_side_effects=True, vmem_limit_bytes=56 * 1024 * 1024
        ),
        cost_estimate=pl.CostEstimate(flops=1 << 30, bytes_accessed=5 << 20, transcendentals=0),
        name="evaluate",
    )(table, traces, mute, operator, wavelet)
    return pl.pallas_call(
        unpack,
        out_shape=jax.ShapeDtypeStruct((2, 2, 32, 1024), F32),
        in_specs=[vmem],
        out_specs=vmem,
        name="unpack",
    )(got)


def solution(mesh):
    in_specs = (P("blk", "freq", None), P("blk", "freq"), P(None, "freq", "blk", None), P())
    out_specs = P(None, "freq", "blk", None)
    return jax.shard_map(body, mesh=mesh, in_specs=in_specs, out_specs=out_specs, check_vma=False)
```

```python
import functools
import math

import jax
import jax.numpy as jnp
import numpy as np
from jax import lax
from jax.experimental import pallas as pl
from jax.experimental.pallas import tpu as pltpu
from jax.sharding import PartitionSpec as P

LOW_FREQ = 8
MESH = pl.DeviceIdType.MESH
BF16 = jnp.bfloat16
F32 = jnp.float32

OFFSETS = (0, 1, 3, 6, 4)


def div(a, b):
    return lax.div(a, jnp.int32(b))


def rem(a, b):
    return lax.rem(a, jnp.int32(b))


def wrap(a, n):
    return jnp.where(a >= n, a - n, a)


def frequency_at(device):
    z, core = device // 2, device % 2
    return (z % 8 + 4) % 8 * 4 + core * 2 + (1 + z // 8 + z % 8 // 4) % 2


def band_table(samples, count):
    times = np.arange(samples, dtype=np.int64)
    freqs = LOW_FREQ + np.array([frequency_at(t) for t in range(count)], dtype=np.int64)
    phase = times[:, None] * freqs[None, :] % samples
    angle = phase.astype(np.float32) * np.float32(2.0 * math.pi / samples)
    factor = np.float32(1.0 / math.sqrt(samples))
    table = np.concatenate([np.cos(angle) * factor, -np.sin(angle) * factor], axis=1)
    return np.ascontiguousarray(table.T).astype(jnp.bfloat16)


def swap(x):
    return pltpu.roll(x, 64, 1)


def low_half(rows):
    return lax.broadcasted_iota(jnp.int32, (rows, 128), 1) < 64


def kernel(
    table_in, traces, mute_in, oper_in, wave_in, got,
    table, mute, oper, wave, tr, zs, zb, pin, mid, pk, xs, xm, xp, w, y, res, gs,
    in_sem, tr_sem, zsend, zrecv, xsend, xrecv, ysend, yrecv, gsend, grecv, asend, arecv, bsend, brecv, csend, crecv,
):
    b = lax.axis_index("blk").astype(jnp.int32)
    f = lax.axis_index("freq").astype(jnp.int32)
    h, xy = div(b, 16), rem(b, 16)
    yy, xx = div(xy, 4), rem(xy, 4)
    l, core = div(f, 2), rem(f, 2)
    z = h * 8 + l
    u = h * 4 + yy
    d = rem(l - u + 8, 8)
    kept = (d == 0) | (d == 1) | (d == 3) | (d == 6) | ((d == 4) & (h == 0))
    slot = jnp.where(d == 1, 1, 0) + jnp.where(d == 3, 2, 0) + jnp.where(d == 6, 3, 0) + jnp.where(d == 4, 4, 0) + 5 * h
    far = rem(l + 4, 8)
    part = rem(1 + h + div(l, 4), 2)
    group = div(xx, 2)
    mine = far * 4 + group * 2 + part
    block = (yy * 2 + rem(xx, 2)) * 2 + core
    far_group = far * 2 + group

    def load(ch):
        return pltpu.make_async_copy(traces.at[pl.ds(8 * ch, 8)], tr.at[pl.ds(8 * ch, 8)], tr_sem.at[ch])

    @pl.when(kept)
    def _():
        load(0).start()

    inputs = [
        pltpu.make_async_copy(src, dst, in_sem.at[i])
        for i, (src, dst) in enumerate(((mute_in, mute), (table_in, table), (oper_in, oper), (wave_in, wave)))
    ]
    for c in inputs:
        c.start()

    @pl.when(kept)
    def _():
        for ch in range(1, 4):
            load(ch).start()

    barrier = pltpu.get_barrier_semaphore()

    def ring_device(to):
        return xy + jnp.where(to >= 8, 16, 0), wrap(to, 8) * 2 + core

    for half in range(2):
        for off in OFFSETS[: 5 - half]:
            to = 8 * half + wrap(yy + (4 * half + off) % 8, 8)

            @pl.when(to != z)
            def _():
                pl.semaphore_signal(barrier, inc=1, device_id=ring_device(to), device_id_type=MESH)

    at_y = [wrap(yy + i, 4) * 4 for i in range(4)]
    at_x = [wrap(xx + i, 4) for i in range(4)]

    def greet(device):
        pl.semaphore_signal(barrier, inc=1, device_id=device, device_id_type=MESH)

    def greet_far(i, carry):
        for half in range(2):
            for xl in range(2):
                to = 16 * half + 4 * i + xl
                greet((to + 2 * core, far * 2))
                greet((to + 2 * core, far * 2 + 1))
        return carry

    lax.fori_loop(0, 4, greet_far, 0)

    def near(dy, dx, to_core):
        return h * 16 + at_y[dy] + at_x[dx], l * 2 + to_core

    def greet_plane(i, carry):
        @pl.when((i != xy) | (core != group))
        def _():
            greet((h * 16 + i, l * 2 + group))

        return carry

    lax.fori_loop(0, 16, greet_plane, 0)
    for half in range(2):
        greet((16 * half + xy, far * 2 + core))
    greet(near(0, 0, 1 - core))
    for i in range(1, 4):
        greet(near(0, i, core))
        greet(near(i, 0, core))

    lo32 = low_half(32)
    for c in inputs:
        c.wait()
    for a in range(2):
        for m in range(8):
            re = oper[0, a, :, 128 * m : 128 * m + 128].astype(F32)
            im = oper[1, a, :, 128 * m : 128 * m + 128].astype(F32)
            xs[2 * m, a] = jnp.where(lo32, re, swap(im)).astype(BF16)
            xs[2 * m + 1, a] = jnp.where(lo32, swap(re), im).astype(BF16)

    @pl.when(kept)
    def _():
        eye = (lax.broadcasted_iota(jnp.int32, (64, 64), 0) == lax.broadcasted_iota(jnp.int32, (64, 64), 1)).astype(F32)
        ones = jnp.ones((64, 128), BF16)
        lane = lax.broadcasted_iota(jnp.int32, (512, 128), 1).astype(F32)
        for ch in range(4):
            starts = [
                (eye * mute[8 * ch + s : 8 * ch + s + 1, :].astype(F32)).astype(BF16) for s in range(8)
            ]
            first = jnp.dot(jnp.concatenate(starts, axis=0), ones, preferred_element_type=F32)
            load(ch).wait()
            head = tr[8 * ch : 8 * ch + 8, :, 0:128].astype(F32).reshape(512, 128)
            head = jnp.where(lane >= first, head, 0.0).astype(BF16)
            tr[8 * ch : 8 * ch + 8, :, 0:128] = head.reshape(8, 64, 128)
            spec = lax.dot_general(
                table[...], tr[8 * ch : 8 * ch + 8].reshape(512, 1024), (((1,), (1,)), ((), ())),
                preferred_element_type=F32,
            )
            for p in range(4):
                re = spec[0:32, 128 * p : 128 * p + 128]
                im = spec[32:64, 128 * p : 128 * p + 128]
                even = jnp.where(lo32, re, swap(im))
                odd = jnp.where(lo32, swap(re), im)
                s = 8 * ch + 2 * p
                for jt in range(4):
                    zs[pl.ds(jt * 256 + s, 8, stride=32), :] = even[8 * jt : 8 * jt + 8]
                    zs[pl.ds(jt * 256 + s + 1, 8, stride=32), :] = odd[8 * jt : 8 * jt + 8]
        zb[...] = zs[...].astype(BF16).reshape(32, 32, 128)

    pl.semaphore_wait(barrier, 57 - jnp.where(core == group, 1, 0) + jnp.where(kept, 15, 0))

    @pl.when(kept)
    def _():
        def send(to):
            pltpu.make_async_remote_copy(
                src_ref=zb.at[pl.ds(2 * to, 2)], dst_ref=pin.at[:, slot], send_sem=zsend, recv_sem=zrecv,
                device_id=ring_device(to), device_id_type=MESH,
            ).start()

        def send_two(i, carry):
            send(wrap(z + 7 - i, 16))
            send(wrap(z + 9 + i, 16))
            return carry

        send(wrap(z + 8, 16))
        lax.fori_loop(0, 7, send_two, 0)
        pltpu.make_async_copy(zb.at[pl.ds(2 * z, 2)], pin.at[:, slot], zrecv).start()

    to_half = [16 * rem(a + 1 + div(far, 4), 2) for a in range(2)]

    for i in range(4):
        for xl in range(2):
            for k in range(2):
                to_x = 2 * core + xl
                src = xs.at[at_y[i] + 2 * xl + k]
                other = (to_x != xx) | (core != k) if i == 0 else core >= 0

                @pl.when(other)
                def _():
                    pltpu.make_async_remote_copy(
                        src_ref=src, dst_ref=xm.at[:, xy], send_sem=xsend, recv_sem=xrecv,
                        device_id=(h * 16 + at_y[i] + to_x, l * 2 + k), device_id_type=MESH,
                    ).start()

                @pl.when(jnp.logical_not(other))
                def _():
                    pltpu.make_async_copy(src, xm.at[:, xy], xrecv).start()

    def move(src, dst, send_sem, recv_sem, device):
        pltpu.make_async_remote_copy(
            src_ref=src, dst_ref=dst, send_sem=send_sem, recv_sem=recv_sem, device_id=device, device_id_type=MESH
        ).start()

    def arrived(ref, sem):
        pltpu.make_async_copy(ref, ref, sem).wait()

    def to_group(src, dst, send_sem, recv_sem):
        for which in range(2):
            for xl in range(2):
                to_x = 2 * which + xl

                @pl.when(xx != to_x)
                def _():
                    move(src.at[which], dst, send_sem, recv_sem, (h * 16 + at_y[0] + to_x, f))

                @pl.when(xx == to_x)
                def _():
                    pltpu.make_async_copy(src.at[which], dst, recv_sem).start()

    def fill(k):
        for row in range(8):
            for n in range(5 - row // 4):
                col = (row + OFFSETS[n]) % 8
                tile = jnp.concatenate([pk[row % 4, k, x, n + 5 * (row // 4)] for x in range(4)], axis=0)
                for c in range(2):
                    at = 256 * col + 128 * c + 64 * k
                    w[128 * row : 128 * row + 128, at : at + 64] = tile[:, 64 * c : 64 * c + 64]
                if col != row:
                    turned = tile.T
                    for c in range(2):
                        w[128 * col + 64 * k : 128 * col + 64 * k + 64, 256 * row + 128 * c : 256 * row + 128 * c + 128] = (
                            turned[64 * c : 64 * c + 64]
                        )

    arrived(pin, zrecv)

    @pl.when(core == 0)
    def _():
        to_group(pin, pk.at[yy, 0, xx], asend, arecv.at[yy, xx])
        for i in (2, 1, 3):
            move(pin.at[group], pk.at[yy, 0, xx], asend, arecv.at[yy, xx], near(i, 0, 0))

    @pl.when(core == 1)
    def _():
        for i in (2, 1, 3):
            move(pin, mid.at[yy], bsend, brecv.at[yy], near(i, 0, 1))
        to_group(pin, pk.at[yy, 1, xx], asend, arecv.at[yy, xx])

    arrived(xm, xrecv)
    for a in range(2):
        move(
            xm.at[a], xp.at[pl.ds(pl.multiple_of(16 * h, 16), 16)], ysend, yrecv,
            (to_half[a] + xy, far * 2 + core),
        )

    def pass_on(row, k):
        for x in range(4):
            arrived(pk.at[row, k, x], arecv.at[row, x])
        rows = pk.at[row, k]
        move(rows, rows, csend, crecv.at[row], near(0, 0, 1 - k))

    others = [div(at_y[i], 4) for i in (1, 3, 2)]

    @pl.when(core == 0)
    def _():
        for n in (1, 3, 2):
            x = at_x[n]
            panel = pk.at[yy, 0, x]
            arrived(panel, arecv.at[yy, x])
            for i in (2, 1, 3):
                move(panel, panel, asend, arecv.at[yy, x], near(i, 0, 0))
        arrived(pk.at[yy, 0, xx], arecv.at[yy, xx])
        move(pk.at[yy, 0], pk.at[yy, 0], csend, crecv.at[yy], near(0, 0, 1))
        for row in others:
            pass_on(row, 0)
        fill(0)
        for row in range(4):
            arrived(pk.at[row, 1], crecv.at[row])
        fill(1)

    @pl.when(core == 1)
    def _():
        for row in others:
            arrived(mid.at[row], brecv.at[row])
            to_group(mid.at[row], pk.at[row, 1, xx], asend, arecv.at[row, xx])
        for row in [yy, *others]:
            pass_on(row, 1)
        fill(1)
        for row in range(4):
            arrived(pk.at[row, 0], crecv.at[row])
        fill(0)

    pltpu.make_async_copy(xp, xp, yrecv).wait()
    lo = low_half(128)
    lane = lax.broadcasted_iota(jnp.int32, (128, 128), 1)
    row_at = lax.broadcasted_iota(jnp.int32, (128, 128), 0)
    for v in range(8):
        x = xp[4 * v : 4 * v + 4].reshape(128, 128).astype(F32)
        sx = swap(x)
        y[256 * v : 256 * v + 128, 0:128] = x.astype(BF16)
        y[256 * v + 128 : 256 * v + 256, 0:128] = jnp.where(lo, -sx, sx).astype(BF16)
        here = row_at + (128 * v - 64 * block)
        y[256 * v : 256 * v + 128, 128:256] = jnp.where(lo & (lane == here), 1.0, 0.0).astype(BF16)
        y[256 * v + 128 : 256 * v + 256, 128:256] = jnp.where(
            (lane >= 64) & (lane - 64 == here), 1.0, 0.0
        ).astype(BF16)
    qr, qi = wave[0, mine], wave[1, mine]
    lo256 = low_half(256)
    for m in range(4):
        rows = slice(256 * m, 256 * m + 256)
        conv = jnp.dot(w[rows], y[...], preferred_element_type=F32)
        x = xp[8 * m : 8 * m + 8].reshape(256, 128).astype(F32)
        sx = swap(x)
        r = conv[:, 128:256] - (qr * x + qi * jnp.where(lo256, -sx, sx)) + conv[:, 0:128]
        res[rows] = r.astype(BF16)

    for v in range(8):
        r = res[128 * v : 128 * v + 128].astype(F32)
        sr = swap(r)
        y[256 * v : 256 * v + 128, 0:128] = r.astype(BF16)
        y[256 * v + 128 : 256 * v + 256, 0:128] = jnp.where(lo, sr, -sr).astype(BF16)
    for half in range(2):
        for at in (512 * half, 512 * half + 256):
            rows = slice(at, at + 256)
            corr = jnp.dot(w[rows], y[:, 0:128], preferred_element_type=F32)
            r = res[rows].astype(F32)
            sr = swap(r)
            g = (corr - (qr * r + qi * jnp.where(lo256, sr, -sr))) * (1.0 / 32.0)
            gs[rows] = g.astype(BF16)

        def send_back(i, carry):
            to = 16 * half + wrap(xy + i, 16)
            pltpu.make_async_remote_copy(
                src_ref=gs.at[pl.ds(pl.multiple_of(to * 32, 32), 32)],
                dst_ref=got.at[part, block],
                send_sem=gsend,
                recv_sem=grecv,
                device_id=(to, far_group),
                device_id_type=MESH,
            ).start()
            return carry

        lax.fori_loop(0, 16, send_back, 0)

    @pl.when(kept)
    def _():
        sent = zb.at[pl.ds(0, 30)]
        pltpu.make_async_copy(sent, sent, zsend).wait()

    pltpu.make_async_copy(xm, xm, ysend).wait()
    most = xs.at[pl.ds(0, 15)]
    pltpu.make_async_copy(most, most, xsend).wait()

    @pl.when(core != group)
    def _():
        pltpu.make_async_copy(xs.at[0], xs.at[0], xsend).wait()

    def left(ref, sem, times):
        for _ in range(times):
            pltpu.make_async_copy(ref, ref, sem).wait()

    left(pin.at[0], asend, 12)
    left(pk.at[0, 0], csend, 4)

    @pl.when(core == 0)
    def _():
        left(pin.at[0], asend, 3)

    @pl.when(core == 1)
    def _():
        left(pin, bsend, 3)

    pltpu.make_async_copy(gs, gs, gsend).wait()
    pltpu.make_async_copy(got, got, grecv).wait()


def unpack(got, out):
    lo = low_half(32)
    for a in range(2):
        for m in range(8):
            left, right = got[a, 2 * m].astype(F32), got[a, 2 * m + 1].astype(F32)
            out[0, a, :, 128 * m : 128 * m + 128] = jnp.where(lo, left, swap(right))
            out[1, a, :, 128 * m : 128 * m + 128] = jnp.where(lo, swap(left), right)


def body(traces, mute, operator, wavelet):
    table = jnp.asarray(band_table(1024, 32))
    vmem = pl.BlockSpec(memory_space=pltpu.VMEM)
    dma = pltpu.SemaphoreType.DMA
    got = pl.pallas_call(
        kernel,
        out_shape=jax.ShapeDtypeStruct((2, 16, 32, 128), BF16),
        in_specs=[pl.BlockSpec(memory_space=pltpu.HBM)] * 5,
        out_specs=vmem,
        scratch_shapes=[
            pltpu.VMEM((64, 1024), BF16),
            pltpu.VMEM((32, 64), jnp.int32),
            pltpu.VMEM((2, 2, 32, 1024), BF16),
            pltpu.SMEM((2, 32), F32),
            pltpu.VMEM((32, 64, 1024), BF16),
            pltpu.VMEM((1024, 128), F32),
            pltpu.VMEM((32, 32, 128), BF16),
            pltpu.VMEM((2, 9, 32, 128), BF16),
            pltpu.VMEM((4, 2, 9, 32, 128), BF16),
            pltpu.VMEM((4, 2, 4, 9, 32, 128), BF16),
            pltpu.VMEM((16, 2, 32, 128), BF16),
            pltpu.VMEM((2, 16, 32, 128), BF16),
            pltpu.VMEM((32, 32, 128), BF16),
            pltpu.VMEM((1024, 2048), BF16),
            pltpu.VMEM((2048, 256), BF16),
            pltpu.VMEM((1024, 128), BF16),
            pltpu.VMEM((1024, 128), BF16),
            dma((4,)), dma((4,)), dma, dma, dma, dma, dma, dma, dma, dma,
            dma, dma((4, 4)), dma, dma((4,)), dma, dma((4,)),
        ],
        compiler_params=pltpu.CompilerParams(
            collective_id=0, has_side_effects=True, vmem_limit_bytes=56 * 1024 * 1024
        ),
        cost_estimate=pl.CostEstimate(flops=1 << 30, bytes_accessed=5 << 20, transcendentals=0),
        name="evaluate",
    )(table, traces, mute, operator, wavelet)
    return pl.pallas_call(
        unpack,
        out_shape=jax.ShapeDtypeStruct((2, 2, 32, 1024), F32),
        in_specs=[vmem],
        out_specs=vmem,
        name="unpack",
    )(got)


def solution(mesh):
    in_specs = (P("blk", "freq", None), P("blk", "freq"), P(None, "freq", "blk", None), P())
    out_specs = P(None, "freq", "blk", None)
    return jax.shard_map(body, mesh=mesh, in_specs=in_specs, out_specs=out_specs, check_vma=False)
```

```python
import functools
import math

import jax
import jax.numpy as jnp
import numpy as np
from jax import lax
from jax.experimental import pallas as pl
from jax.experimental.pallas import tpu as pltpu
from jax.sharding import PartitionSpec as P

LOW_FREQ = 8
MESH = pl.DeviceIdType.MESH
BF16 = jnp.bfloat16
F32 = jnp.float32

OFFSETS = (0, 1, 3, 6, 4)


def div(a, b):
    return lax.div(a, jnp.int32(b))


def rem(a, b):
    return lax.rem(a, jnp.int32(b))


def wrap(a, n):
    return jnp.where(a >= n, a - n, a)


def frequency_at(device):
    z, core = device // 2, device % 2
    return (z % 8 + 4) % 8 * 4 + core * 2 + (1 + z // 8 + z % 8 // 4) % 2


def band_table(samples, count):
    times = np.arange(samples, dtype=np.int64)
    freqs = LOW_FREQ + np.array([frequency_at(t) for t in range(count)], dtype=np.int64)
    phase = times[:, None] * freqs[None, :] % samples
    angle = phase.astype(np.float32) * np.float32(2.0 * math.pi / samples)
    factor = np.float32(1.0 / math.sqrt(samples))
    table = np.concatenate([np.cos(angle) * factor, -np.sin(angle) * factor], axis=1)
    return np.ascontiguousarray(table.T).astype(jnp.bfloat16)


def swap(x):
    return pltpu.roll(x, 64, 1)


def low_half(rows):
    return lax.broadcasted_iota(jnp.int32, (rows, 128), 1) < 64


def kernel(
    table_in, traces, mute_in, oper_in, wave_in, got,
    table, mute, oper, wave, tr, zs, zb, pin, mid, pk, xs, xm, xp, w, y, res, gs,
    in_sem, tr_sem, zsend, zrecv, xsend, xrecv, ysend, yrecv, gsend, grecv, asend, arecv, bsend, brecv, csend, crecv,
):
    b = lax.axis_index("blk").astype(jnp.int32)
    f = lax.axis_index("freq").astype(jnp.int32)
    h, xy = div(b, 16), rem(b, 16)
    yy, xx = div(xy, 4), rem(xy, 4)
    l, core = div(f, 2), rem(f, 2)
    z = h * 8 + l
    u = h * 4 + yy
    d = rem(l - u + 8, 8)
    kept = (d == 0) | (d == 1) | (d == 3) | (d == 6) | ((d == 4) & (h == 0))
    slot = jnp.where(d == 1, 1, 0) + jnp.where(d == 3, 2, 0) + jnp.where(d == 6, 3, 0) + jnp.where(d == 4, 4, 0) + 5 * h
    far = rem(l + 4, 8)
    part = rem(1 + h + div(l, 4), 2)
    group = div(xx, 2)
    mine = far * 4 + group * 2 + part
    block = (yy * 2 + rem(xx, 2)) * 2 + core
    far_group = far * 2 + group

    def load(ch):
        return pltpu.make_async_copy(traces.at[pl.ds(8 * ch, 8)], tr.at[pl.ds(8 * ch, 8)], tr_sem.at[ch])

    @pl.when(kept)
    def _():
        load(0).start()

    inputs = [
        pltpu.make_async_copy(src, dst, in_sem.at[i])
        for i, (src, dst) in enumerate(((mute_in, mute), (table_in, table), (oper_in, oper), (wave_in, wave)))
    ]
    for c in inputs:
        c.start()

    @pl.when(kept)
    def _():
        for ch in range(1, 4):
            load(ch).start()

    barrier = pltpu.get_barrier_semaphore()

    def ring_device(to):
        return xy + jnp.where(to >= 8, 16, 0), wrap(to, 8) * 2 + core

    for half in range(2):
        for off in OFFSETS[: 5 - half]:
            to = 8 * half + wrap(yy + (4 * half + off) % 8, 8)

            @pl.when(to != z)
            def _():
                pl.semaphore_signal(barrier, inc=1, device_id=ring_device(to), device_id_type=MESH)

    at_y = [wrap(yy + i, 4) * 4 for i in range(4)]
    at_x = [wrap(xx + i, 4) for i in range(4)]

    def greet(device):
        pl.semaphore_signal(barrier, inc=1, device_id=device, device_id_type=MESH)

    def greet_far(i, carry):
        for half in range(2):
            for xl in range(2):
                to = 16 * half + 4 * i + xl
                greet((to + 2 * core, far * 2))
                greet((to + 2 * core, far * 2 + 1))
        return carry

    lax.fori_loop(0, 4, greet_far, 0)

    def near(dy, dx, to_core):
        return h * 16 + at_y[dy] + at_x[dx], l * 2 + to_core

    def greet_plane(i, carry):
        @pl.when((i != xy) | (core != group))
        def _():
            greet((h * 16 + i, l * 2 + group))

        return carry

    lax.fori_loop(0, 16, greet_plane, 0)
    for half in range(2):
        greet((16 * half + xy, far * 2 + core))
    greet(near(0, 0, 1 - core))
    for i in range(1, 4):
        greet(near(0, i, core))
        greet(near(i, 0, core))

    lo32 = low_half(32)
    for c in inputs:
        c.wait()
    for a in range(2):
        for m in range(8):
            re = oper[0, a, :, 128 * m : 128 * m + 128].astype(F32)
            im = oper[1, a, :, 128 * m : 128 * m + 128].astype(F32)
            xs[2 * m, a] = jnp.where(lo32, re, swap(im)).astype(BF16)
            xs[2 * m + 1, a] = jnp.where(lo32, swap(re), im).astype(BF16)

    @pl.when(kept)
    def _():
        eye = (lax.broadcasted_iota(jnp.int32, (64, 64), 0) == lax.broadcasted_iota(jnp.int32, (64, 64), 1)).astype(F32)
        ones = jnp.ones((64, 128), BF16)
        lane = lax.broadcasted_iota(jnp.int32, (512, 128), 1).astype(F32)
        for ch in range(4):
            starts = [
                (eye * mute[8 * ch + s : 8 * ch + s + 1, :].astype(F32)).astype(BF16) for s in range(8)
            ]
            first = jnp.dot(jnp.concatenate(starts, axis=0), ones, preferred_element_type=F32)
            load(ch).wait()
            head = tr[8 * ch : 8 * ch + 8, :, 0:128].astype(F32).reshape(512, 128)
            head = jnp.where(lane >= first, head, 0.0).astype(BF16)
            tr[8 * ch : 8 * ch + 8, :, 0:128] = head.reshape(8, 64, 128)
            spec = lax.dot_general(
                table[...], tr[8 * ch : 8 * ch + 8].reshape(512, 1024), (((1,), (1,)), ((), ())),
                preferred_element_type=F32,
            )
            for p in range(4):
                re = spec[0:32, 128 * p : 128 * p + 128]
                im = spec[32:64, 128 * p : 128 * p + 128]
                even = jnp.where(lo32, re, swap(im))
                odd = jnp.where(lo32, swap(re), im)
                s = 8 * ch + 2 * p
                for jt in range(4):
                    zs[pl.ds(jt * 256 + s, 8, stride=32), :] = even[8 * jt : 8 * jt + 8]
                    zs[pl.ds(jt * 256 + s + 1, 8, stride=32), :] = odd[8 * jt : 8 * jt + 8]
        zb[...] = zs[...].astype(BF16).reshape(32, 32, 128)

    pl.semaphore_wait(barrier, 57 - jnp.where(core == group, 1, 0) + jnp.where(kept, 15, 0))

    @pl.when(kept)
    def _():
        def send(to):
            pltpu.make_async_remote_copy(
                src_ref=zb.at[pl.ds(2 * to, 2)], dst_ref=pin.at[:, slot], send_sem=zsend, recv_sem=zrecv,
                device_id=ring_device(to), device_id_type=MESH,
            ).start()

        def send_two(i, carry):
            for to in (wrap(z + 7 - i, 16), wrap(z + 9 + i, 16)):

                @pl.when((to != 4) & (to != 12))
                def _():
                    send(to)

            return carry

        for to in (4, 12):

            @pl.when(z != to)
            def _():
                send(jnp.int32(to))

        @pl.when((z != 4) & (z != 12))
        def _():
            send(wrap(z + 8, 16))

        lax.fori_loop(0, 7, send_two, 0)
        pltpu.make_async_copy(zb.at[pl.ds(2 * z, 2)], pin.at[:, slot], zrecv).start()

    to_half = [16 * rem(a + 1 + div(far, 4), 2) for a in range(2)]

    for i in range(4):
        for xl in range(2):
            for k in range(2):
                to_x = 2 * core + xl
                src = xs.at[at_y[i] + 2 * xl + k]
                other = (to_x != xx) | (core != k) if i == 0 else core >= 0

                @pl.when(other)
                def _():
                    pltpu.make_async_remote_copy(
                        src_ref=src, dst_ref=xm.at[:, xy], send_sem=xsend, recv_sem=xrecv,
                        device_id=(h * 16 + at_y[i] + to_x, l * 2 + k), device_id_type=MESH,
                    ).start()

                @pl.when(jnp.logical_not(other))
                def _():
                    pltpu.make_async_copy(src, xm.at[:, xy], xrecv).start()

    def move(src, dst, send_sem, recv_sem, device):
        pltpu.make_async_remote_copy(
            src_ref=src, dst_ref=dst, send_sem=send_sem, recv_sem=recv_sem, device_id=device, device_id_type=MESH
        ).start()

    def arrived(ref, sem):
        pltpu.make_async_copy(ref, ref, sem).wait()

    def to_group(src, dst, send_sem, recv_sem):
        for which in range(2):
            for xl in range(2):
                to_x = 2 * which + xl

                @pl.when(xx != to_x)
                def _():
                    move(src.at[which], dst, send_sem, recv_sem, (h * 16 + at_y[0] + to_x, f))

                @pl.when(xx == to_x)
                def _():
                    pltpu.make_async_copy(src.at[which], dst, recv_sem).start()

    def fill(k):
        for row in range(8):
            for n in range(5 - row // 4):
                col = (row + OFFSETS[n]) % 8
                tile = jnp.concatenate([pk[row % 4, k, x, n + 5 * (row // 4)] for x in range(4)], axis=0)
                for c in range(2):
                    at = 256 * col + 128 * c + 64 * k
                    w[128 * row : 128 * row + 128, at : at + 64] = tile[:, 64 * c : 64 * c + 64]
                if col != row:
                    turned = tile.T
                    for c in range(2):
                        w[128 * col + 64 * k : 128 * col + 64 * k + 64, 256 * row + 128 * c : 256 * row + 128 * c + 128] = (
                            turned[64 * c : 64 * c + 64]
                        )

    arrived(pin, zrecv)

    @pl.when(core == 0)
    def _():
        to_group(pin, pk.at[yy, 0, xx], asend, arecv.at[yy, xx])
        for i in (2, 1, 3):
            move(pin.at[group], pk.at[yy, 0, xx], asend, arecv.at[yy, xx], near(i, 0, 0))

    @pl.when(core == 1)
    def _():
        for i in (2, 1, 3):
            move(pin, mid.at[yy], bsend, brecv.at[yy], near(i, 0, 1))
        to_group(pin, pk.at[yy, 1, xx], asend, arecv.at[yy, xx])

    arrived(xm, xrecv)
    for a in range(2):
        move(
            xm.at[a], xp.at[pl.ds(pl.multiple_of(16 * h, 16), 16)], ysend, yrecv,
            (to_half[a] + xy, far * 2 + core),
        )

    def pass_on(row, k):
        for x in range(4):
            arrived(pk.at[row, k, x], arecv.at[row, x])
        rows = pk.at[row, k]
        move(rows, rows, csend, crecv.at[row], near(0, 0, 1 - k))

    others = [div(at_y[i], 4) for i in (1, 3, 2)]

    @pl.when(core == 0)
    def _():
        for n in (1, 3, 2):
            x = at_x[n]
            panel = pk.at[yy, 0, x]
            arrived(panel, arecv.at[yy, x])
            for i in (2, 1, 3):
                move(panel, panel, asend, arecv.at[yy, x], near(i, 0, 0))
        arrived(pk.at[yy, 0, xx], arecv.at[yy, xx])
        move(pk.at[yy, 0], pk.at[yy, 0], csend, crecv.at[yy], near(0, 0, 1))
        for row in others:
            pass_on(row, 0)
        fill(0)
        for row in range(4):
            arrived(pk.at[row, 1], crecv.at[row])
        fill(1)

    @pl.when(core == 1)
    def _():
        for row in others:
            arrived(mid.at[row], brecv.at[row])
            to_group(mid.at[row], pk.at[row, 1, xx], asend, arecv.at[row, xx])
        for row in [yy, *others]:
            pass_on(row, 1)
        fill(1)
        for row in range(4):
            arrived(pk.at[row, 0], crecv.at[row])
        fill(0)

    pltpu.make_async_copy(xp, xp, yrecv).wait()
    lo = low_half(128)
    lane = lax.broadcasted_iota(jnp.int32, (128, 128), 1)
    row_at = lax.broadcasted_iota(jnp.int32, (128, 128), 0)
    for v in range(8):
        x = xp[4 * v : 4 * v + 4].reshape(128, 128).astype(F32)
        sx = swap(x)
        y[256 * v : 256 * v + 128, 0:128] = x.astype(BF16)
        y[256 * v + 128 : 256 * v + 256, 0:128] = jnp.where(lo, -sx, sx).astype(BF16)
        here = row_at + (128 * v - 64 * block)
        y[256 * v : 256 * v + 128, 128:256] = jnp.where(lo & (lane == here), 1.0, 0.0).astype(BF16)
        y[256 * v + 128 : 256 * v + 256, 128:256] = jnp.where(
            (lane >= 64) & (lane - 64 == here), 1.0, 0.0
        ).astype(BF16)
    qr, qi = wave[0, mine], wave[1, mine]
    lo256 = low_half(256)
    for m in range(4):
        rows = slice(256 * m, 256 * m + 256)
        conv = jnp.dot(w[rows], y[...], preferred_element_type=F32)
        x = xp[8 * m : 8 * m + 8].reshape(256, 128).astype(F32)
        sx = swap(x)
        r = conv[:, 128:256] - (qr * x + qi * jnp.where(lo256, -sx, sx)) + conv[:, 0:128]
        res[rows] = r.astype(BF16)

    for v in range(8):
        r = res[128 * v : 128 * v + 128].astype(F32)
        sr = swap(r)
        y[256 * v : 256 * v + 128, 0:128] = r.astype(BF16)
        y[256 * v + 128 : 256 * v + 256, 0:128] = jnp.where(lo, sr, -sr).astype(BF16)
    for at in (0, 256, 512, 768):
        rows = slice(at, at + 256)
        corr = jnp.dot(w[rows], y[:, 0:128], preferred_element_type=F32)
        r = res[rows].astype(F32)
        sr = swap(r)
        g = (corr - (qr * r + qi * jnp.where(lo256, sr, -sr))) * (1.0 / 32.0)
        gs[rows] = g.astype(BF16)

        def send_back(i, carry):
            to = at // 32 + wrap(rem(xy, 8) + i, 8)
            pltpu.make_async_remote_copy(
                src_ref=gs.at[pl.ds(pl.multiple_of(to * 32, 32), 32)],
                dst_ref=got.at[part, block],
                send_sem=gsend,
                recv_sem=grecv,
                device_id=(to, far_group),
                device_id_type=MESH,
            ).start()
            return carry

        lax.fori_loop(0, 8, send_back, 0)

    @pl.when(kept)
    def _():
        sent = zb.at[pl.ds(0, 30)]
        pltpu.make_async_copy(sent, sent, zsend).wait()

    pltpu.make_async_copy(xm, xm, ysend).wait()
    most = xs.at[pl.ds(0, 15)]
    pltpu.make_async_copy(most, most, xsend).wait()

    @pl.when(core != group)
    def _():
        pltpu.make_async_copy(xs.at[0], xs.at[0], xsend).wait()

    def left(ref, sem, times):
        for _ in range(times):
            pltpu.make_async_copy(ref, ref, sem).wait()

    left(pin.at[0], asend, 12)
    left(pk.at[0, 0], csend, 4)

    @pl.when(core == 0)
    def _():
        left(pin.at[0], asend, 3)

    @pl.when(core == 1)
    def _():
        left(pin, bsend, 3)

    pltpu.make_async_copy(gs, gs, gsend).wait()
    pltpu.make_async_copy(got, got, grecv).wait()


def unpack(got, out):
    lo = low_half(32)
    for a in range(2):
        for m in range(8):
            left, right = got[a, 2 * m].astype(F32), got[a, 2 * m + 1].astype(F32)
            out[0, a, :, 128 * m : 128 * m + 128] = jnp.where(lo, left, swap(right))
            out[1, a, :, 128 * m : 128 * m + 128] = jnp.where(lo, swap(left), right)


def body(traces, mute, operator, wavelet):
    table = jnp.asarray(band_table(1024, 32))
    vmem = pl.BlockSpec(memory_space=pltpu.VMEM)
    dma = pltpu.SemaphoreType.DMA
    got = pl.pallas_call(
        kernel,
        out_shape=jax.ShapeDtypeStruct((2, 16, 32, 128), BF16),
        in_specs=[pl.BlockSpec(memory_space=pltpu.HBM)] * 5,
        out_specs=vmem,
        scratch_shapes=[
            pltpu.VMEM((64, 1024), BF16),
            pltpu.VMEM((32, 64), jnp.int32),
            pltpu.VMEM((2, 2, 32, 1024), BF16),
            pltpu.SMEM((2, 32), F32),
            pltpu.VMEM((32, 64, 1024), BF16),
            pltpu.VMEM((1024, 128), F32),
            pltpu.VMEM((32, 32, 128), BF16),
            pltpu.VMEM((2, 9, 32, 128), BF16),
            pltpu.VMEM((4, 2, 9, 32, 128), BF16),
            pltpu.VMEM((4, 2, 4, 9, 32, 128), BF16),
            pltpu.VMEM((16, 2, 32, 128), BF16),
            pltpu.VMEM((2, 16, 32, 128), BF16),
            pltpu.VMEM((32, 32, 128), BF16),
            pltpu.VMEM((1024, 2048), BF16),
            pltpu.VMEM((2048, 256), BF16),
            pltpu.VMEM((1024, 128), BF16),
            pltpu.VMEM((1024, 128), BF16),
            dma((4,)), dma((4,)), dma, dma, dma, dma, dma, dma, dma, dma,
            dma, dma((4, 4)), dma, dma((4,)), dma, dma((4,)),
        ],
        compiler_params=pltpu.CompilerParams(
            collective_id=0, has_side_effects=True, vmem_limit_bytes=56 * 1024 * 1024
        ),
        cost_estimate=pl.CostEstimate(flops=1 << 30, bytes_accessed=5 << 20, transcendentals=0),
        name="evaluate",
    )(table, traces, mute, operator, wavelet)
    return pl.pallas_call(
        unpack,
        out_shape=jax.ShapeDtypeStruct((2, 2, 32, 1024), F32),
        in_specs=[vmem],
        out_specs=vmem,
        name="unpack",
    )(got)


def solution(mesh):
    in_specs = (P("blk", "freq", None), P("blk", "freq"), P(None, "freq", "blk", None), P())
    out_specs = P(None, "freq", "blk", None)
    return jax.shard_map(body, mesh=mesh, in_specs=in_specs, out_specs=out_specs, check_vma=False)
```

```python
import functools
import math

import jax
import jax.numpy as jnp
import numpy as np
from jax import lax
from jax.experimental import pallas as pl
from jax.experimental.pallas import tpu as pltpu
from jax.sharding import PartitionSpec as P

LOW_FREQ = 8
MESH = pl.DeviceIdType.MESH
BF16 = jnp.bfloat16
F32 = jnp.float32

OFFSETS = (0, 1, 3, 6, 4)


def div(a, b):
    return lax.div(a, jnp.int32(b))


def rem(a, b):
    return lax.rem(a, jnp.int32(b))


def wrap(a, n):
    return jnp.where(a >= n, a - n, a)


def frequency_at(device):
    z, core = device // 2, device % 2
    return (z % 8 + 4) % 8 * 4 + core * 2 + (1 + z // 8 + z % 8 // 4) % 2


def band_table(samples, count):
    times = np.arange(samples, dtype=np.int64)
    freqs = LOW_FREQ + np.array([frequency_at(t) for t in range(count)], dtype=np.int64)
    phase = times[:, None] * freqs[None, :] % samples
    angle = phase.astype(np.float32) * np.float32(2.0 * math.pi / samples)
    factor = np.float32(1.0 / math.sqrt(samples))
    table = np.concatenate([np.cos(angle) * factor, -np.sin(angle) * factor], axis=1)
    return np.ascontiguousarray(table.T).astype(jnp.bfloat16)


def swap(x):
    return pltpu.roll(x, 64, 1)


def low_half(rows):
    return lax.broadcasted_iota(jnp.int32, (rows, 128), 1) < 64


def kernel(
    table_in, traces, mute_in, oper_in, wave_in, got,
    table, mute, oper, wave, tr, zs, zb, pin, mid, pk, xs, xm, xp, w, y, res, gs,
    in_sem, tr_sem, zsend, zrecv, xsend, xrecv, ysend, yrecv, gsend, grecv, asend, arecv, bsend, brecv, csend, crecv,
):
    b = lax.axis_index("blk").astype(jnp.int32)
    f = lax.axis_index("freq").astype(jnp.int32)
    h, xy = div(b, 16), rem(b, 16)
    yy, xx = div(xy, 4), rem(xy, 4)
    l, core = div(f, 2), rem(f, 2)
    z = h * 8 + l
    u = h * 4 + yy
    d = rem(l - u + 8, 8)
    kept = (d == 0) | (d == 1) | (d == 3) | (d == 6) | ((d == 4) & (h == 0))
    slot = jnp.where(d == 1, 1, 0) + jnp.where(d == 3, 2, 0) + jnp.where(d == 6, 3, 0) + jnp.where(d == 4, 4, 0) + 5 * h
    far = rem(l + 4, 8)
    part = rem(1 + h + div(l, 4), 2)
    group = div(xx, 2)
    mine = far * 4 + group * 2 + part
    block = (yy * 2 + rem(xx, 2)) * 2 + core
    far_group = far * 2 + group

    def load(ch):
        return pltpu.make_async_copy(traces.at[pl.ds(8 * ch, 8)], tr.at[pl.ds(8 * ch, 8)], tr_sem.at[ch])

    @pl.when(kept)
    def _():
        load(0).start()

    inputs = [
        pltpu.make_async_copy(src, dst, in_sem.at[i])
        for i, (src, dst) in enumerate(((mute_in, mute), (table_in, table), (oper_in, oper), (wave_in, wave)))
    ]
    for c in inputs:
        c.start()

    @pl.when(kept)
    def _():
        for ch in range(1, 4):
            load(ch).start()

    barrier = pltpu.get_barrier_semaphore()

    def ring_device(to):
        return xy + jnp.where(to >= 8, 16, 0), wrap(to, 8) * 2 + core

    for half in range(2):
        for off in OFFSETS[: 5 - half]:
            to = 8 * half + wrap(yy + (4 * half + off) % 8, 8)

            @pl.when(to != z)
            def _():
                pl.semaphore_signal(barrier, inc=1, device_id=ring_device(to), device_id_type=MESH)

    at_y = [wrap(yy + i, 4) * 4 for i in range(4)]
    at_x = [wrap(xx + i, 4) for i in range(4)]

    def greet(device):
        pl.semaphore_signal(barrier, inc=1, device_id=device, device_id_type=MESH)

    def greet_far(i, carry):
        for half in range(2):
            for xl in range(2):
                to = 16 * half + 4 * i + xl
                greet((to + 2 * core, far * 2))
                greet((to + 2 * core, far * 2 + 1))
        return carry

    lax.fori_loop(0, 4, greet_far, 0)

    def near(dy, dx, to_core):
        return h * 16 + at_y[dy] + at_x[dx], l * 2 + to_core

    def greet_plane(i, carry):
        @pl.when((i != xy) | (core != group))
        def _():
            greet((h * 16 + i, l * 2 + group))

        return carry

    lax.fori_loop(0, 16, greet_plane, 0)
    for half in range(2):
        greet((16 * half + xy, far * 2 + core))
    greet(near(0, 0, 1 - core))
    for i in range(1, 4):
        greet(near(0, i, core))
        greet(near(i, 0, core))

    lo32 = low_half(32)
    for c in inputs:
        c.wait()
    for a in range(2):
        for m in range(8):
            re = oper[0, a, :, 128 * m : 128 * m + 128].astype(F32)
            im = oper[1, a, :, 128 * m : 128 * m + 128].astype(F32)
            xs[2 * m, a] = jnp.where(lo32, re, swap(im)).astype(BF16)
            xs[2 * m + 1, a] = jnp.where(lo32, swap(re), im).astype(BF16)

    @pl.when(kept)
    def _():
        eye = (lax.broadcasted_iota(jnp.int32, (64, 64), 0) == lax.broadcasted_iota(jnp.int32, (64, 64), 1)).astype(F32)
        ones = jnp.ones((64, 128), BF16)
        lane = lax.broadcasted_iota(jnp.int32, (512, 128), 1).astype(F32)
        for ch in range(4):
            starts = [
                (eye * mute[8 * ch + s : 8 * ch + s + 1, :].astype(F32)).astype(BF16) for s in range(8)
            ]
            first = jnp.dot(jnp.concatenate(starts, axis=0), ones, preferred_element_type=F32)
            load(ch).wait()
            head = tr[8 * ch : 8 * ch + 8, :, 0:128].astype(F32).reshape(512, 128)
            head = jnp.where(lane >= first, head, 0.0).astype(BF16)
            tr[8 * ch : 8 * ch + 8, :, 0:128] = head.reshape(8, 64, 128)
            spec = lax.dot_general(
                table[...], tr[8 * ch : 8 * ch + 8].reshape(512, 1024), (((1,), (1,)), ((), ())),
                preferred_element_type=F32,
            )
            for p in range(4):
                re = spec[0:32, 128 * p : 128 * p + 128]
                im = spec[32:64, 128 * p : 128 * p + 128]
                even = jnp.where(lo32, re, swap(im))
                odd = jnp.where(lo32, swap(re), im)
                s = 8 * ch + 2 * p
                for jt in range(4):
                    zs[pl.ds(jt * 256 + s, 8, stride=32), :] = even[8 * jt : 8 * jt + 8]
                    zs[pl.ds(jt * 256 + s + 1, 8, stride=32), :] = odd[8 * jt : 8 * jt + 8]
        zb[...] = zs[0:1024].astype(BF16).reshape(32, 32, 128)

    pl.semaphore_wait(barrier, 57 - jnp.where(core == group, 1, 0) + jnp.where(kept, 15, 0))

    @pl.when(kept)
    def _():
        def send(to):
            pltpu.make_async_remote_copy(
                src_ref=zb.at[pl.ds(2 * to, 2)], dst_ref=pin.at[:, slot], send_sem=zsend, recv_sem=zrecv,
                device_id=ring_device(to), device_id_type=MESH,
            ).start()

        def send_two(i, carry):
            for to in (wrap(z + 7 - i, 16), wrap(z + 9 + i, 16)):

                @pl.when((to != 4) & (to != 12))
                def _():
                    send(to)

            return carry

        for to in (4, 12):

            @pl.when(z != to)
            def _():
                send(jnp.int32(to))

        @pl.when((z != 4) & (z != 12))
        def _():
            send(wrap(z + 8, 16))

        lax.fori_loop(0, 7, send_two, 0)
        pltpu.make_async_copy(zb.at[pl.ds(2 * z, 2)], pin.at[:, slot], zrecv).start()

    to_half = [16 * rem(a + 1 + div(far, 4), 2) for a in range(2)]

    for i in range(4):
        for xl in range(2):
            for k in range(2):
                to_x = 2 * core + xl
                src = xs.at[at_y[i] + 2 * xl + k]
                other = (to_x != xx) | (core != k) if i == 0 else core >= 0

                @pl.when(other)
                def _():
                    pltpu.make_async_remote_copy(
                        src_ref=src, dst_ref=xm.at[:, xy], send_sem=xsend, recv_sem=xrecv,
                        device_id=(h * 16 + at_y[i] + to_x, l * 2 + k), device_id_type=MESH,
                    ).start()

                @pl.when(jnp.logical_not(other))
                def _():
                    pltpu.make_async_copy(src, xm.at[:, xy], xrecv).start()

    def move(src, dst, send_sem, recv_sem, device):
        pltpu.make_async_remote_copy(
            src_ref=src, dst_ref=dst, send_sem=send_sem, recv_sem=recv_sem, device_id=device, device_id_type=MESH
        ).start()

    def arrived(ref, sem):
        pltpu.make_async_copy(ref, ref, sem).wait()

    def to_group(src, dst, send_sem, recv_sem):
        for which in range(2):
            for xl in range(2):
                to_x = 2 * which + xl

                @pl.when(xx != to_x)
                def _():
                    move(src.at[which], dst, send_sem, recv_sem, (h * 16 + at_y[0] + to_x, f))

                @pl.when(xx == to_x)
                def _():
                    pltpu.make_async_copy(src.at[which], dst, recv_sem).start()

    def fill(k):
        for row in range(8):
            for n in range(5 - row // 4):
                col = (row + OFFSETS[n]) % 8
                tile = jnp.concatenate([pk[row % 4, k, x, n + 5 * (row // 4)] for x in range(4)], axis=0)
                for c in range(2):
                    at = 256 * col + 128 * c + 64 * k
                    w[128 * row : 128 * row + 128, at : at + 64] = tile[:, 64 * c : 64 * c + 64]
                if col != row:
                    turned = tile.T
                    for c in range(2):
                        w[128 * col + 64 * k : 128 * col + 64 * k + 64, 256 * row + 128 * c : 256 * row + 128 * c + 128] = (
                            turned[64 * c : 64 * c + 64]
                        )

    arrived(pin, zrecv)

    @pl.when(core == 0)
    def _():
        to_group(pin, pk.at[yy, 0, xx], asend, arecv.at[yy, xx])
        for i in (2, 1, 3):
            move(pin.at[group], pk.at[yy, 0, xx], asend, arecv.at[yy, xx], near(i, 0, 0))

    @pl.when(core == 1)
    def _():
        for i in (2, 1, 3):
            move(pin, mid.at[yy], bsend, brecv.at[yy], near(i, 0, 1))
        to_group(pin, pk.at[yy, 1, xx], asend, arecv.at[yy, xx])

    arrived(xm, xrecv)
    for a in range(2):
        move(
            xm.at[a], xp.at[pl.ds(pl.multiple_of(16 * h, 16), 16)], ysend, yrecv,
            (to_half[a] + xy, far * 2 + core),
        )

    def pass_on(row, k):
        for x in range(4):
            arrived(pk.at[row, k, x], arecv.at[row, x])
        rows = pk.at[row, k]
        move(rows, rows, csend, crecv.at[row], near(0, 0, 1 - k))

    others = [div(at_y[i], 4) for i in (1, 3, 2)]

    @pl.when(core == 0)
    def _():
        for n in (1, 3, 2):
            x = at_x[n]
            panel = pk.at[yy, 0, x]
            arrived(panel, arecv.at[yy, x])
            for i in (2, 1, 3):
                move(panel, panel, asend, arecv.at[yy, x], near(i, 0, 0))
        arrived(pk.at[yy, 0, xx], arecv.at[yy, xx])
        move(pk.at[yy, 0], pk.at[yy, 0], csend, crecv.at[yy], near(0, 0, 1))
        for row in others:
            pass_on(row, 0)
        fill(0)
        for row in range(4):
            arrived(pk.at[row, 1], crecv.at[row])
        fill(1)

    @pl.when(core == 1)
    def _():
        for row in others:
            arrived(mid.at[row], brecv.at[row])
            to_group(mid.at[row], pk.at[row, 1, xx], asend, arecv.at[row, xx])
        for row in [yy, *others]:
            pass_on(row, 1)
        fill(1)
        for row in range(4):
            arrived(pk.at[row, 0], crecv.at[row])
        fill(0)

    pltpu.make_async_copy(xp, xp, yrecv).wait()
    lo = low_half(128)
    lane = lax.broadcasted_iota(jnp.int32, (128, 128), 1)
    row_at = lax.broadcasted_iota(jnp.int32, (128, 128), 0)
    for v in range(8):
        x = xp[4 * v : 4 * v + 4].reshape(128, 128).astype(F32)
        sx = swap(x)
        y[256 * v : 256 * v + 128, 0:128] = x.astype(BF16)
        y[256 * v + 128 : 256 * v + 256, 0:128] = jnp.where(lo, -sx, sx).astype(BF16)
        here = row_at + (128 * v - 64 * block)
        y[256 * v : 256 * v + 128, 128:256] = jnp.where(lo & (lane == here), 1.0, 0.0).astype(BF16)
        y[256 * v + 128 : 256 * v + 256, 128:256] = jnp.where(
            (lane >= 64) & (lane - 64 == here), 1.0, 0.0
        ).astype(BF16)
    qr, qi = wave[0, mine], wave[1, mine]
    lo256 = low_half(256)
    for m in range(4):
        rows = slice(256 * m, 256 * m + 256)
        conv = jnp.dot(w[rows], y[...], preferred_element_type=F32)
        x = xp[8 * m : 8 * m + 8].reshape(256, 128).astype(F32)
        sx = swap(x)
        r = conv[:, 128:256] - (qr * x + qi * jnp.where(lo256, -sx, sx)) + conv[:, 0:128]
        res[rows] = r.astype(BF16)

    for v in range(8):
        r = res[128 * v : 128 * v + 128].astype(F32)
        sr = swap(r)
        y[256 * v : 256 * v + 128, 0:128] = r.astype(BF16)
        y[256 * v + 128 : 256 * v + 256, 0:128] = jnp.where(lo, sr, -sr).astype(BF16)
    for at in (0, 256, 512, 768):
        rows = slice(at, at + 256)
        corr = jnp.dot(w[rows], y[:, 0:128], preferred_element_type=F32)
        r = res[rows].astype(F32)
        sr = swap(r)
        g = (corr - (qr * r + qi * jnp.where(lo256, sr, -sr))) * (1.0 / 32.0)
        gs[rows] = g.astype(BF16)

        def send_back(i, carry):
            to = at // 32 + wrap(rem(xy, 8) + i, 8)
            pltpu.make_async_remote_copy(
                src_ref=gs.at[pl.ds(pl.multiple_of(to * 32, 32), 32)],
                dst_ref=got.at[part, block],
                send_sem=gsend,
                recv_sem=grecv,
                device_id=(to, far_group),
                device_id_type=MESH,
            ).start()
            return carry

        lax.fori_loop(0, 8, send_back, 0)

    @pl.when(kept)
    def _():
        sent = zb.at[pl.ds(0, 30)]
        pltpu.make_async_copy(sent, sent, zsend).wait()

    pltpu.make_async_copy(xm, xm, ysend).wait()
    most = xs.at[pl.ds(0, 15)]
    pltpu.make_async_copy(most, most, xsend).wait()

    @pl.when(core != group)
    def _():
        pltpu.make_async_copy(xs.at[0], xs.at[0], xsend).wait()

    def left(ref, sem, times):
        for _ in range(times):
            pltpu.make_async_copy(ref, ref, sem).wait()

    left(pin.at[0], asend, 12)
    left(pk.at[0, 0], csend, 4)

    @pl.when(core == 0)
    def _():
        left(pin.at[0], asend, 3)

    @pl.when(core == 1)
    def _():
        left(pin, bsend, 3)

    pltpu.make_async_copy(gs, gs, gsend).wait()
    pltpu.make_async_copy(got, got, grecv).wait()


def unpack(got, out):
    lo = low_half(32)
    for a in range(2):
        for m in range(8):
            left, right = got[a, 2 * m].astype(F32), got[a, 2 * m + 1].astype(F32)
            out[0, a, :, 128 * m : 128 * m + 128] = jnp.where(lo, left, swap(right))
            out[1, a, :, 128 * m : 128 * m + 128] = jnp.where(lo, swap(left), right)


def body(traces, mute, operator, wavelet):
    table = jnp.asarray(band_table(1024, 32))
    vmem = pl.BlockSpec(memory_space=pltpu.VMEM)
    dma = pltpu.SemaphoreType.DMA
    got = pl.pallas_call(
        kernel,
        out_shape=jax.ShapeDtypeStruct((2, 16, 32, 128), BF16),
        in_specs=[pl.BlockSpec(memory_space=pltpu.HBM)] * 5,
        out_specs=vmem,
        scratch_shapes=[
            pltpu.VMEM((64, 1024), BF16),
            pltpu.VMEM((32, 64), jnp.int32),
            pltpu.VMEM((2, 2, 32, 1024), BF16),
            pltpu.SMEM((2, 32), F32),
            pltpu.VMEM((32, 64, 1024), BF16),
            pltpu.VMEM((1056, 128), F32),
            pltpu.VMEM((32, 32, 128), BF16),
            pltpu.VMEM((2, 9, 32, 128), BF16),
            pltpu.VMEM((4, 2, 9, 32, 128), BF16),
            pltpu.VMEM((4, 2, 4, 9, 32, 128), BF16),
            pltpu.VMEM((16, 2, 32, 128), BF16),
            pltpu.VMEM((2, 16, 32, 128), BF16),
            pltpu.VMEM((32, 32, 128), BF16),
            pltpu.VMEM((1024, 2048), BF16),
            pltpu.VMEM((2048, 256), BF16),
            pltpu.VMEM((1024, 128), BF16),
            pltpu.VMEM((1024, 128), BF16),
            dma((4,)), dma((4,)), dma, dma, dma, dma, dma, dma, dma, dma,
            dma, dma((4, 4)), dma, dma((4,)), dma, dma((4,)),
        ],
        compiler_params=pltpu.CompilerParams(
            collective_id=0, has_side_effects=True, vmem_limit_bytes=56 * 1024 * 1024
        ),
        cost_estimate=pl.CostEstimate(flops=1 << 30, bytes_accessed=5 << 20, transcendentals=0),
        name="evaluate",
    )(table, traces, mute, operator, wavelet)
    return pl.pallas_call(
        unpack,
        out_shape=jax.ShapeDtypeStruct((2, 2, 32, 1024), F32),
        in_specs=[vmem],
        out_specs=vmem,
        name="unpack",
    )(got)


def solution(mesh):
    in_specs = (P("blk", "freq", None), P("blk", "freq"), P(None, "freq", "blk", None), P())
    out_specs = P(None, "freq", "blk", None)
    return jax.shard_map(body, mesh=mesh, in_specs=in_specs, out_specs=out_specs, check_vma=False)
```
